32 devices in a mesh: grp: 2 (over y), hor: 8 (over z, x), blk: 2 (over core).
Axes of the slice: x: 2, y: 2, z: 4, core: 2. Of those that a mesh axis runs over, the one named last changes fastest.
Arguments:
- hessian_part: float32 [16, 1024, 512], P(('grp', 'hor'), 'blk'), parts along dimension 0, as said below
- coupling: float32 [16, 512, 512], P(('grp', 'hor'), None, 'blk'), parts along dimension 0, may hold values from -1 to 1, as said below
- rhs: float32 [16, 512, 256], P(('grp', 'hor'), None, 'blk'), parts along dimension 0, may hold values from -6 to 6
Outputs:
- reduced_diag: float32 [16, 512, 512], P(('grp', 'hor'), None, 'blk'), parts along dimension 0
- reduced_coupling: float32 [16, 512, 512], P(('grp', 'hor'), None, 'blk'), parts along dimension 0
- reduced_rhs: float32 [16, 512, 256], P(('grp', 'hor'), None, 'blk'), parts along dimension 0
The draws below stay inside these ranges and needn't reach their ends.
There are 2 independent parts, one for each index of `grp`. The reference program is written for one: setup_inputs(seed, part) draws one part's arguments, and reference() takes and returns one part's arrays. A program takes and returns all parts, laid end to end along the dimension named above; each array names one. Nothing has to cross between parts.
Inputs may be any that keep to these rules, and one draw needn't show every extreme that they name: `hessian_part`: each partial block is symmetric positive definite. `coupling`: together with the summed Hessian blocks, the block tridiagonal matrix of all 8 sections is symmetric positive definite.
All inputs are finite; a program needn't handle non-finite values.
Results may differ from the reference program's by a relative error of at most 0.0003.
Values sent between devices are 32-bit elements; how exact they have to be, the bound alone decides.
A program may use at most 64 MiB of HBM per device.

```python
import jax
import jax.numpy as jnp
from jax import lax

NS = 512
NRHS = 256
LEVELS = 2
SECTIONS = 8
N_BLK = 2


def draw_hessian_part(key, part):
    key = jax.random.fold_in(key, 11)
    factor_key, diag_key, direction_key, strength_key = jax.random.split(key, 4)
    shape = (SECTIONS, N_BLK, NS, NS)
    low_shape = (SECTIONS, N_BLK, NS, 4)
    factors = jax.random.truncated_normal(factor_key, -4.0, 4.0, shape, jnp.float32)
    directions = jax.random.truncated_normal(direction_key, -4.0, 4.0, low_shape, jnp.float32)
    outer = jnp.einsum('spij,spkj->spik', factors, factors, precision=lax.Precision.HIGHEST) / (8.0 * NS)
    directions = directions * NS ** (-0.5)
    strength = jnp.exp(jax.random.uniform(strength_key, (SECTIONS, N_BLK), jnp.float32, 1.7917595, 3.1780538))
    dense = jnp.einsum('spik,spjk->spij', directions, directions, precision=lax.Precision.HIGHEST)
    total = outer + strength[..., None, None] * dense
    symmetric = 0.5 * (total + jnp.swapaxes(total, 2, 3))
    diagonal = jax.random.uniform(diag_key, (SECTIONS, N_BLK, NS), jnp.float32, 1.0, 1.1)
    blocks = symmetric + diagonal[..., None] * jnp.eye(NS, dtype=jnp.float32)
    return blocks.reshape(SECTIONS, N_BLK * NS, NS).astype(jnp.float32)


def draw_coupling(key, part):
    key = jax.random.fold_in(key, 23)
    diag_key, noise_key = jax.random.split(key)
    shape = (SECTIONS, NS, NS)
    noise = jax.random.truncated_normal(noise_key, -3.5, 3.5, shape, jnp.float32)
    dominant = jax.random.uniform(diag_key, (SECTIONS, NS), jnp.float32, 0.7, 0.9)
    blocks = noise * (0.04 * NS ** (-0.5)) + dominant[..., None] * jnp.eye(NS, dtype=jnp.float32)
    return blocks.astype(jnp.float32)


def steps_of(rng, extent, shards, low, largest):
    def one(axis_at, blocks):
        heights = jax.random.uniform(jax.random.fold_in(jax.random.fold_in(rng, 6), axis_at), (blocks,), jnp.float32, low / len(shards), largest / len(shards))
        return jnp.repeat(jnp.exp(heights), extent[axis_at] // blocks).reshape((-1,) + (1,) * (len(extent) - axis_at - 1))

    level = one(*shards[0])
    for cut in shards[1:]:
        level = level * one(*cut)
    return level


def centred(stream_key, shape, width, most, cuts=(), kind=jnp.bfloat16):
    gain = steps_of(stream_key, shape, cuts, -0.22, 0.18) if cuts else 1.0
    array = jax.random.normal(stream_key, shape, jnp.float32) * width * gain
    return jnp.minimum(jnp.maximum(array, -most), most).astype(kind)


def setup_inputs(seed: int = 0, part: int = 0) -> dict:
    splits = jax.random.split(jax.random.key(seed), 4)
    own_keys = jax.random.split(jax.random.fold_in(splits[3], part), 4)
    return {
        "hessian_part": draw_hessian_part(jax.random.fold_in(jax.random.fold_in(splits[3], part), 71), part),
        "coupling": draw_coupling(jax.random.fold_in(jax.random.fold_in(splits[3], part), 71), part),
        "rhs": centred(own_keys[2], (SECTIONS, NS, NRHS), 1.0, 6.0, ((0, 8), (2, 2)), jnp.float32),
    }


def shift_lower(values, distance):
    return jnp.concatenate([jnp.zeros_like(values[:distance]), values[:-distance]], 0)

def shift_upper(values, distance):
    return jnp.concatenate([values[distance:], jnp.zeros_like(values[:distance])], 0)

def batched(form, left, right):
    return jnp.einsum(form, left, right, precision=lax.Precision.HIGHEST)

def reference(hessian_part, coupling, rhs):
    sections = hessian_part.shape[0]
    diag = jnp.sum(hessian_part.reshape(sections, N_BLK, NS, NS), axis=1)
    section_index = jnp.arange(sections)
    link = jnp.where((section_index >= 1)[:, None, None], coupling, jnp.zeros_like(coupling))
    right = rhs
    identity = jnp.broadcast_to(jnp.eye(NS, dtype=jnp.float32), diag.shape)
    for depth in range(LEVELS):
        distance = 2 ** depth
        factor = jnp.linalg.cholesky(diag)
        inverse = lax.linalg.triangular_solve(factor, identity, left_side=True, lower=True)
        product = batched('sij,sjk->sik', inverse, link)
        scaled = batched('sij,sjk->sik', inverse, right)
        inverse_low = shift_lower(inverse, distance)
        product_low = shift_lower(product, distance)
        scaled_low = shift_lower(scaled, distance)
        product_high = shift_upper(product, distance)
        scaled_high = shift_upper(scaled, distance)
        gram = batched('sij,skj->sik', link, inverse_low)
        new_diag = diag - batched('sij,skj->sik', gram, gram) - batched('sji,sjk->sik', product_high, product_high)
        new_link = -batched('sij,sjk->sik', gram, product_low)
        new_right = right - batched('sij,sjk->sik', gram, scaled_low) - batched('sji,sjk->sik', product_high, scaled_high)
        diag, link, right = (new_diag, new_link, new_right)
    return (diag, link, right)
```

```python
import functools

import jax
import jax.numpy as jnp
from jax import lax
from jax.experimental import pallas as pl
from jax.experimental.pallas import tpu as pltpu
from jax.sharding import PartitionSpec as P

LEVELS = 2
ROWS = 8
BASE = 128
NN = (((1,), (0,)), ((), ()))
NT = (((1,), (1,)), ((), ()))
TN = (((0,), (0,)), ((), ()))


def split(x):
    high = x.astype(jnp.bfloat16)
    return high, (x - high.astype(jnp.float32)).astype(jnp.bfloat16)


def multiply(a, b, dims=NN):
    dot = functools.partial(lax.dot_general, dimension_numbers=dims, preferred_element_type=jnp.float32)
    return dot(a[0], b[0]) + (dot(a[0], b[1]) + dot(a[1], b[0]))


def sweep_base(tiles):
    width = tiles[0].shape[1]
    shape = (ROWS, width)
    lane = lax.broadcasted_iota(jnp.int32, shape, 1)
    sub = lax.broadcasted_iota(jnp.int32, shape, 0)
    count = len(tiles)
    for p in range(count):
        first = p * ROWS
        block = tiles[p]
        columns = [
            [jnp.broadcast_to(tiles[q][:, first + l : first + l + 1], shape) for l in range(ROWS)] for q in range(count)
        ]
        e = {
            (i, j): jnp.broadcast_to(columns[p][j][i : i + 1, :], shape) for i in range(ROWS) for j in range(i + 1)
        }
        at = lambda i, j: (max(i, j), min(i, j))
        for k in range(ROWS):
            inv = 1.0 / e[k, k]
            others = [i for i in range(ROWS) if i != k]
            col = {i: e[at(i, k)] for i in others}
            scaled = {i: col[i] * inv for i in others}
            for i in others:
                for j in others:
                    if j <= i:
                        e[i, j] = e[i, j] - scaled[i] * col[j]
            for i in others:
                e[at(i, k)] = scaled[i]
            e[k, k] = -inv
        negated = []
        for l in range(ROWS):
            value = e[at(0, l)]
            for i in range(1, ROWS):
                value = jnp.where(sub == i, e[at(i, l)], value)
            negated.append(value)
        rows = None
        for l in range(ROWS):
            term = negated[l] * jnp.broadcast_to(block[l : l + 1, :], shape)
            rows = -term if rows is None else rows - term
        for l in range(ROWS):
            rows = jnp.where(lane == first + l, negated[l], rows)
        spread = [jnp.broadcast_to(rows[l : l + 1, :], shape) for l in range(ROWS)]
        inside = (lane >= first) & (lane < first + ROWS)
        for q in range(count):
            if q == p:
                continue
            value = jnp.where(inside, 0.0, tiles[q])
            for l in range(ROWS):
                value = value - columns[q][l] * spread[l]
            tiles[q] = value
        tiles[p] = rows
    return tiles


def sweep_all(work, base):
    order = work.shape[0]

    def step(k, carry):
        start = pl.multiple_of(k * BASE, BASE)
        tiles = [work[pl.ds(pl.multiple_of(start + r * ROWS, ROWS), ROWS), pl.ds(start, BASE)] for r in range(BASE // ROWS)]
        for r, tile in enumerate(sweep_base(tiles)):
            base[pl.ds(r * ROWS, ROWS), :] = tile
        negated = base[...]
        panel = split(work[:, pl.ds(start, BASE)])
        rows = -multiply(split(negated), split(work[pl.ds(start, BASE), :]))
        work[pl.ds(start, BASE), :] = rows
        work[pl.ds(start, BASE), pl.ds(start, BASE)] = negated
        rows = work[pl.ds(start, BASE), :]
        work[:, pl.ds(start, BASE)] = jnp.zeros((order, BASE), jnp.float32)
        work[...] = work[...] - multiply(panel, split(rows))
        work[pl.ds(start, BASE), :] = rows
        return carry

    lax.fori_loop(0, order // BASE, step, 0)


def invert_pair_kernel(a_ref, b_ref, total_ref, out_ref, work, base):
    total_ref[...] = a_ref[...] + b_ref[...]
    work[...] = total_ref[...]
    sweep_all(work, base)
    out_ref[...] = work[...]


def invert_kernel(a_ref, out_ref, work, base):
    work[...] = a_ref[...]
    sweep_all(work, base)
    out_ref[...] = work[...]


VMEM = pl.BlockSpec(memory_space=pltpu.VMEM)


def local_call(kernel, ins, outs, scratch, flops, name):
    return pl.pallas_call(
        kernel,
        out_shape=[jax.ShapeDtypeStruct(s, jnp.float32) for s in outs],
        in_specs=[VMEM] * len(ins),
        out_specs=[VMEM] * len(outs),
        scratch_shapes=scratch,
        compiler_params=pltpu.CompilerParams(vmem_limit_bytes=48 * 2**20),
        cost_estimate=pl.CostEstimate(flops=flops, bytes_accessed=4 * 2**20, transcendentals=0),
        name=name,
    )(*ins)


def invert(ins, order):
    scratch = [pltpu.VMEM((order, order), jnp.float32), pltpu.VMEM((BASE, BASE), jnp.float32)]
    square = (order, order)
    if len(ins) == 2:
        return local_call(invert_pair_kernel, ins, [square, square], scratch, 40 * 10**9, "sum_invert")
    return [ins[0], local_call(invert_kernel, ins, [square], scratch, 40 * 10**9, "invert")[0]]


def join(target, mine, other, index, axis):
    half = mine.shape[axis]
    for value, at in ((mine, index), (other, 1 - index)):
        place = pl.ds(pl.multiple_of(at * half, half), half)
        if axis:
            target[:, place] = value[...]
        else:
            target[place, :] = value[...]


def update_kernel(
    last, diag, low_a, low_b, high_a, high_b, link_a, link_b, next_a, next_b, link_low, right_low, right_high, right,
    new_diag, new_link, new_right, low, high, link, nxt,
):
    index = lax.axis_index("blk")
    half = link_low.shape[1]
    join(low, low_a, low_b, index, 0)
    join(high, high_a, high_b, index, 0)
    join(link, link_a, link_b, index, 1)
    join(nxt, next_a, next_b, index, 1)
    mine = pl.ds(pl.multiple_of(index * half, half), half)
    low_pair = split(low[...])
    high_pair = split(high[...])
    link_pair = split(link[...])
    next_pair = split(nxt[...])
    link_rows = split(link[mine, :]) if last else link_pair
    next_columns = split(nxt[:, mine]) if last else next_pair
    old = diag[:, mine] if last else diag[...]
    gram = split(multiply(low_pair, link_rows, NT))
    upper = split(multiply(high_pair, next_columns))
    new_diag[...] = old + multiply(link_pair, gram) + multiply(next_pair, upper, TN)
    new_link[...] = multiply(link_pair, split(multiply(low_pair, split(link_low[...]))))
    scaled_low = split(multiply(low_pair, split(right_low[...])))
    scaled_high = split(multiply(high_pair, split(right_high[...])))
    new_right[...] = right[...] + multiply(link_pair, scaled_low) + multiply(next_pair, scaled_high, TN)


def shifted(block, axis, distance):
    devices = range(lax.axis_size(axis))
    route = [(i - distance, i) for i in devices if i - distance in devices]
    return lax.ppermute(block, axis, route)


def swapped(block):
    return lax.ppermute(block, "blk", [(0, 1), (1, 0)])


def shards(hessian_part, coupling, rhs):
    order = coupling.shape[1]
    half = coupling.shape[2]
    blk_index = lax.axis_index("blk")
    section_index = lax.axis_index("hor")
    link = coupling[0]
    link = jnp.where(section_index >= 1, link, jnp.zeros_like(link))
    right = rhs[0]
    ins = [hessian_part[0], swapped(hessian_part[0])]
    for depth in range(LEVELS):
        last = depth == LEVELS - 1
        distance = 2**depth
        next_link = shifted(link, "hor", -distance)
        link_low = shifted(link, "hor", distance)
        right_low = shifted(right, "hor", distance)
        right_high = shifted(right, "hor", -distance)
        link_other = swapped(link)
        next_other = swapped(next_link)
        diag, negated = invert(ins, order)
        mine = lax.dynamic_slice_in_dim(negated, blk_index * half, half, 0)
        low = shifted(mine, "hor", distance)
        high = shifted(mine, "hor", -distance)
        low_other = swapped(low)
        high_other = swapped(high)
        square = pltpu.VMEM((order, order), jnp.float32)
        args = [diag, low, low_other, high, high_other, link, link_other, next_link, next_other]
        args += [link_low, right_low, right_high, right]
        shape = (order, half) if last else (order, order)
        diag, link, right = local_call(
            functools.partial(update_kernel, last), args, [shape, (order, half), right.shape], [square] * 4, 3 * 10**9, "update"
        )
        ins = [diag]
    return (diag[None], link[None], right[None])


def solution(mesh):
    spec = P(("grp", "hor"), None, "blk")
    return jax.shard_map(
        shards,
        mesh=mesh,
        in_specs=(P(("grp", "hor"), "blk", None), spec, spec),
        out_specs=(spec, spec, spec),
        check_vma=False,
    )
```

```python
import functools

import jax
import jax.numpy as jnp
from jax import lax
from jax.experimental import pallas as pl
from jax.experimental.pallas import tpu as pltpu
from jax.sharding import PartitionSpec as P

LEVELS = 2
ROWS = 8
BASE = 128
NN = (((1,), (0,)), ((), ()))
NT = (((1,), (1,)), ((), ()))
TN = (((0,), (0,)), ((), ()))


def split(x):
    high = x.astype(jnp.bfloat16)
    return high, (x - high.astype(jnp.float32)).astype(jnp.bfloat16)


def multiply(a, b, dims=NN):
    dot = functools.partial(lax.dot_general, dimension_numbers=dims, preferred_element_type=jnp.float32)
    return dot(a[0], b[0]) + (dot(a[0], b[1]) + dot(a[1], b[0]))


def sweep_base(tiles):
    width = tiles[0].shape[1]
    shape = (ROWS, width)
    lane = lax.broadcasted_iota(jnp.int32, shape, 1)
    sub = lax.broadcasted_iota(jnp.int32, shape, 0)
    count = len(tiles)
    for p in range(count):
        first = p * ROWS
        block = tiles[p]
        columns = [
            [jnp.broadcast_to(tiles[q][:, first + l : first + l + 1], shape) for l in range(ROWS)] for q in range(count)
        ]
        e = {
            (i, j): jnp.broadcast_to(columns[p][j][i : i + 1, :], shape) for i in range(ROWS) for j in range(i + 1)
        }
        at = lambda i, j: (max(i, j), min(i, j))
        for k in range(ROWS):
            inv = 1.0 / e[k, k]
            others = [i for i in range(ROWS) if i != k]
            col = {i: e[at(i, k)] for i in others}
            scaled = {i: col[i] * inv for i in others}
            for i in others:
                for j in others:
                    if j <= i:
                        e[i, j] = e[i, j] - scaled[i] * col[j]
            for i in others:
                e[at(i, k)] = scaled[i]
            e[k, k] = -inv
        negated = []
        for l in range(ROWS):
            value = e[at(0, l)]
            for i in range(1, ROWS):
                value = jnp.where(sub == i, e[at(i, l)], value)
            negated.append(value)
        rows = None
        for l in range(ROWS):
            term = negated[l] * jnp.broadcast_to(block[l : l + 1, :], shape)
            rows = -term if rows is None else rows - term
        for l in range(ROWS):
            rows = jnp.where(lane == first + l, negated[l], rows)
        spread = [jnp.broadcast_to(rows[l : l + 1, :], shape) for l in range(ROWS)]
        inside = (lane >= first) & (lane < first + ROWS)
        for q in range(count):
            if q == p:
                continue
            value = jnp.where(inside, 0.0, tiles[q])
            for l in range(ROWS):
                value = value - columns[q][l] * spread[l]
            tiles[q] = value
        tiles[p] = rows
    return tiles


def sweep_all(work, base):
    order = work.shape[0]

    def step(k, carry):
        start = pl.multiple_of(k * BASE, BASE)
        tiles = [work[pl.ds(pl.multiple_of(start + r * ROWS, ROWS), ROWS), pl.ds(start, BASE)] for r in range(BASE // ROWS)]
        for r, tile in enumerate(sweep_base(tiles)):
            base[pl.ds(r * ROWS, ROWS), :] = tile
        negated = base[...]
        panel = split(work[:, pl.ds(start, BASE)])
        rows = -multiply(split(negated), split(work[pl.ds(start, BASE), :]))
        work[pl.ds(start, BASE), :] = rows
        work[pl.ds(start, BASE), pl.ds(start, BASE)] = negated
        rows = work[pl.ds(start, BASE), :]
        work[:, pl.ds(start, BASE)] = jnp.zeros((order, BASE), jnp.float32)
        work[...] = work[...] - multiply(panel, split(rows))
        work[pl.ds(start, BASE), :] = rows
        return carry

    lax.fori_loop(0, order // BASE, step, 0)


def lower_blocks(order):
    count = order // BASE
    return [(i, j) for i in range(count) for j in range(i + 1)]


def pack_half(out_ref, work):
    blocks = lower_blocks(work.shape[0])
    half = len(blocks) // 2
    first = lax.axis_index("blk") == 0
    for n in range(half):
        (i, j), (k, l) = blocks[n], blocks[half + n]
        mine = work[i * BASE : (i + 1) * BASE, j * BASE : (j + 1) * BASE]
        other = work[k * BASE : (k + 1) * BASE, l * BASE : (l + 1) * BASE]
        out_ref[n * BASE : (n + 1) * BASE, :] = jnp.where(first, mine, other)


def invert_pair_kernel(a_ref, b_ref, total_ref, out_ref, work, base):
    total_ref[...] = a_ref[...] + b_ref[...]
    work[...] = total_ref[...]
    sweep_all(work, base)
    pack_half(out_ref, work)


def invert_kernel(a_ref, out_ref, work, base):
    work[...] = a_ref[...]
    sweep_all(work, base)
    pack_half(out_ref, work)


def gate_kernel(*refs):
    pass


def gated(packed, others):
    return pl.pallas_call(
        gate_kernel,
        out_shape=jax.ShapeDtypeStruct(packed.shape, packed.dtype),
        in_specs=[pl.BlockSpec(memory_space=pl.ANY)] * (1 + len(others)),
        out_specs=pl.BlockSpec(memory_space=pl.ANY),
        input_output_aliases={0: 0},
        name="gate",
    )(packed, *others)


VMEM = pl.BlockSpec(memory_space=pltpu.VMEM)


def local_call(kernel, ins, outs, scratch, flops, name):
    return pl.pallas_call(
        kernel,
        out_shape=[jax.ShapeDtypeStruct(s, jnp.float32) for s in outs],
        in_specs=[VMEM] * len(ins),
        out_specs=[VMEM] * len(outs),
        scratch_shapes=scratch,
        compiler_params=pltpu.CompilerParams(vmem_limit_bytes=48 * 2**20),
        cost_estimate=pl.CostEstimate(flops=flops, bytes_accessed=4 * 2**20, transcendentals=0),
        name=name,
    )(*ins)


def invert(ins, order):
    scratch = [pltpu.VMEM((order, order), jnp.float32), pltpu.VMEM((BASE, BASE), jnp.float32)]
    square = (order, order)
    packed = (len(lower_blocks(order)) // 2 * BASE, BASE)
    if len(ins) == 2:
        return local_call(invert_pair_kernel, ins, [square, packed], scratch, 40 * 10**9, "sum_invert")
    return [ins[0], local_call(invert_kernel, ins, [packed], scratch, 40 * 10**9, "invert")[0]]


def join(target, mine, other, index):
    half = mine.shape[1]
    for value, at in ((mine, index), (other, 1 - index)):
        target[:, pl.ds(pl.multiple_of(at * half, half), half)] = value[...]


def unpack(target, mine, other, index):
    blocks = lower_blocks(target.shape[0])
    half = len(blocks) // 2
    for n, (i, j) in enumerate(blocks):
        place = slice(n % half * BASE, (n % half + 1) * BASE)
        block = jnp.where(index == n // half, mine[place, :], other[place, :])
        target[i * BASE : (i + 1) * BASE, j * BASE : (j + 1) * BASE] = block
        if i != j:
            target[j * BASE : (j + 1) * BASE, i * BASE : (i + 1) * BASE] = block.T


def update_kernel(
    last, diag, low_a, low_b, high_a, high_b, link_a, link_b, next_a, next_b, link_low, right_low, right_high, right,
    new_diag, new_link, new_right, low, high, link, nxt,
):
    index = lax.axis_index("blk")
    half = link_low.shape[1]
    unpack(low, low_a, low_b, index)
    unpack(high, high_a, high_b, index)
    join(link, link_a, link_b, index)
    join(nxt, next_a, next_b, index)
    mine = pl.ds(pl.multiple_of(index * half, half), half)
    low_pair = split(low[...])
    high_pair = split(high[...])
    link_pair = split(link[...])
    next_pair = split(nxt[...])
    link_rows = split(link[mine, :]) if last else link_pair
    next_columns = split(nxt[:, mine]) if last else next_pair
    old = diag[:, mine] if last else diag[...]
    gram = split(multiply(low_pair, link_rows, NT))
    upper = split(multiply(high_pair, next_columns))
    new_diag[...] = old + multiply(link_pair, gram) + multiply(next_pair, upper, TN)
    new_link[...] = multiply(link_pair, split(multiply(low_pair, split(link_low[...]))))
    scaled_low = split(multiply(low_pair, split(right_low[...])))
    scaled_high = split(multiply(high_pair, split(right_high[...])))
    new_right[...] = right[...] + multiply(link_pair, scaled_low) + multiply(next_pair, scaled_high, TN)


def shifted(block, axis, distance):
    devices = range(lax.axis_size(axis))
    route = [(i - distance, i) for i in devices if i - distance in devices]
    return lax.ppermute(block, axis, route)


def swapped(block):
    return lax.ppermute(block, "blk", [(0, 1), (1, 0)])


def shards(hessian_part, coupling, rhs):
    order = coupling.shape[1]
    half = coupling.shape[2]
    section_index = lax.axis_index("hor")
    link = coupling[0]
    link = jnp.where(section_index >= 1, link, jnp.zeros_like(link))
    right = rhs[0]
    ins = [hessian_part[0], swapped(hessian_part[0])]
    for depth in range(LEVELS):
        last = depth == LEVELS - 1
        distance = 2**depth
        next_link = shifted(link, "hor", -distance)
        link_low = shifted(link, "hor", distance)
        right_low = shifted(right, "hor", distance)
        right_high = shifted(right, "hor", -distance)
        link_other = swapped(link)
        next_other = swapped(next_link)
        diag, mine = invert(ins, order)
        mine = gated(mine, [next_link, link_low, right_low, right_high, link_other])
        low = shifted(mine, "hor", distance)
        high = shifted(mine, "hor", -distance)
        low_other = swapped(low)
        high_other = swapped(high)
        square = pltpu.VMEM((order, order), jnp.float32)
        args = [diag, low, low_other, high, high_other, link, link_other, next_link, next_other]
        args += [link_low, right_low, right_high, right]
        shape = (order, half) if last else (order, order)
        diag, link, right = local_call(
            functools.partial(update_kernel, last), args, [shape, (order, half), right.shape], [square] * 4, 3 * 10**9, "update"
        )
        ins = [diag]
    return (diag[None], link[None], right[None])


def solution(mesh):
    spec = P(("grp", "hor"), None, "blk")
    return jax.shard_map(
        shards,
        mesh=mesh,
        in_specs=(P(("grp", "hor"), "blk", None), spec, spec),
        out_specs=(spec, spec, spec),
        check_vma=False,
    )
```

```python
import functools

import jax
import jax.numpy as jnp
from jax import lax
from jax.experimental import pallas as pl
from jax.experimental.pallas import tpu as pltpu
from jax.sharding import PartitionSpec as P

LEVELS = 2
ROWS = 8
BASE = 128
NN = (((1,), (0,)), ((), ()))
NT = (((1,), (1,)), ((), ()))
TN = (((0,), (0,)), ((), ()))


def split(x):
    high = x.astype(jnp.bfloat16)
    return high, (x - high.astype(jnp.float32)).astype(jnp.bfloat16)


def multiply(a, b, dims=NN):
    dot = functools.partial(lax.dot_general, dimension_numbers=dims, preferred_element_type=jnp.float32)
    return dot(a[0], b[0]) + (dot(a[0], b[1]) + dot(a[1], b[0]))


def sweep_base(tiles):
    width = tiles[0].shape[1]
    shape = (ROWS, width)
    lane = lax.broadcasted_iota(jnp.int32, shape, 1)
    sub = lax.broadcasted_iota(jnp.int32, shape, 0)
    count = len(tiles)
    for p in range(count):
        first = p * ROWS
        block = tiles[p]
        columns = [
            [jnp.broadcast_to(tiles[q][:, first + l : first + l + 1], shape) for l in range(ROWS)]
            for q in range(p, min(p + 2, count))
        ]
        e = {
            (i, j): jnp.broadcast_to(columns[0][j][i : i + 1, :], shape) for i in range(ROWS) for j in range(i + 1)
        }
        at = lambda i, j: (max(i, j), min(i, j))
        for k in range(ROWS):
            inv = 1.0 / e[k, k]
            others = [i for i in range(ROWS) if i != k]
            col = {i: e[at(i, k)] for i in others}
            scaled = {i: col[i] * inv for i in others}
            for i in others:
                for j in others:
                    if j <= i:
                        e[i, j] = e[i, j] - scaled[i] * col[j]
            for i in others:
                e[at(i, k)] = scaled[i]
            e[k, k] = -inv
        negated = []
        for l in range(ROWS):
            value = e[at(0, l)]
            for i in range(1, ROWS):
                value = jnp.where(sub == i, e[at(i, l)], value)
            negated.append(value)
        rows = None
        for l in range(ROWS):
            term = negated[l] * jnp.broadcast_to(block[l : l + 1, :], shape)
            rows = -term if rows is None else rows - term
        for l in range(ROWS):
            rows = jnp.where(lane == first + l, negated[l], rows)
        spread = [jnp.broadcast_to(rows[l : l + 1, :], shape) for l in range(ROWS)]
        inside = (lane >= first) & (lane < first + ROWS)
        panel = jnp.concatenate([jnp.where(inside, tile, 0.0) for tile in tiles], 0)
        zero = jnp.zeros(shape, jnp.float32)
        padded = jnp.concatenate([rows if q == p else zero for q in range(count)], 0)
        delta = multiply(split(panel), split(padded))
        for q in range(count):
            if q == p:
                continue
            value = jnp.where(inside, 0.0, tiles[q])
            if q == p + 1:
                for l in range(ROWS):
                    value = value - columns[1][l] * spread[l]
            else:
                value = value - delta[q * ROWS : (q + 1) * ROWS, :]
            tiles[q] = value
        tiles[p] = rows
    return tiles


def sweep_all(work, base):
    order = work.shape[0]

    def step(k, carry):
        start = pl.multiple_of(k * BASE, BASE)
        tiles = [work[pl.ds(pl.multiple_of(start + r * ROWS, ROWS), ROWS), pl.ds(start, BASE)] for r in range(BASE // ROWS)]
        for r, tile in enumerate(sweep_base(tiles)):
            base[pl.ds(r * ROWS, ROWS), :] = tile
        negated = base[...]
        panel = split(work[:, pl.ds(start, BASE)])
        rows = -multiply(split(negated), split(work[pl.ds(start, BASE), :]))
        work[pl.ds(start, BASE), :] = rows
        work[pl.ds(start, BASE), pl.ds(start, BASE)] = negated
        rows = work[pl.ds(start, BASE), :]
        work[:, pl.ds(start, BASE)] = jnp.zeros((order, BASE), jnp.float32)
        work[...] = work[...] - multiply(panel, split(rows))
        work[pl.ds(start, BASE), :] = rows
        return carry

    lax.fori_loop(0, order // BASE, step, 0)


def lower_blocks(order):
    count = order // BASE
    return [(i, j) for i in range(count) for j in range(i + 1)]


def pack_half(out_ref, work):
    blocks = lower_blocks(work.shape[0])
    half = len(blocks) // 2
    first = lax.axis_index("blk") == 0
    for n in range(half):
        (i, j), (k, l) = blocks[n], blocks[half + n]
        mine = work[i * BASE : (i + 1) * BASE, j * BASE : (j + 1) * BASE]
        other = work[k * BASE : (k + 1) * BASE, l * BASE : (l + 1) * BASE]
        out_ref[n * BASE : (n + 1) * BASE, :] = jnp.where(first, mine, other)


def invert_pair_kernel(a_ref, b_ref, total_ref, out_ref, work, base):
    total_ref[...] = a_ref[...] + b_ref[...]
    work[...] = total_ref[...]
    sweep_all(work, base)
    pack_half(out_ref, work)


def invert_kernel(a_ref, out_ref, work, base):
    work[...] = a_ref[...]
    sweep_all(work, base)
    pack_half(out_ref, work)


def gate_kernel(*refs):
    pass


def gated(packed, others):
    return pl.pallas_call(
        gate_kernel,
        out_shape=jax.ShapeDtypeStruct(packed.shape, packed.dtype),
        in_specs=[pl.BlockSpec(memory_space=pl.ANY)] * (1 + len(others)),
        out_specs=pl.BlockSpec(memory_space=pl.ANY),
        input_output_aliases={0: 0},
        name="gate",
    )(packed, *others)


VMEM = pl.BlockSpec(memory_space=pltpu.VMEM)


def local_call(kernel, ins, outs, scratch, flops, name, mib):
    return pl.pallas_call(
        kernel,
        out_shape=[jax.ShapeDtypeStruct(s, jnp.float32) for s in outs],
        in_specs=[VMEM] * len(ins),
        out_specs=[VMEM] * len(outs),
        scratch_shapes=scratch,
        compiler_params=pltpu.CompilerParams(vmem_limit_bytes=mib * 2**20),
        cost_estimate=pl.CostEstimate(flops=flops, bytes_accessed=4 * 2**20, transcendentals=0),
        name=name,
    )(*ins)


def invert(ins, order):
    scratch = [pltpu.VMEM((order, order), jnp.float32), pltpu.VMEM((BASE, BASE), jnp.float32)]
    square = (order, order)
    packed = (len(lower_blocks(order)) // 2 * BASE, BASE)
    if len(ins) == 2:
        return local_call(invert_pair_kernel, ins, [square, packed], scratch, 40 * 10**9, "sum_invert", 20)
    return [ins[0], local_call(invert_kernel, ins, [packed], scratch, 40 * 10**9, "invert", 20)[0]]


def join(target, mine, other, index):
    half = mine.shape[1]
    for value, at in ((mine, index), (other, 1 - index)):
        target[:, pl.ds(pl.multiple_of(at * half, half), half)] = value[...]


def unpack(target, mine, other, index):
    blocks = lower_blocks(target.shape[0])
    half = len(blocks) // 2
    for n, (i, j) in enumerate(blocks):
        place = slice(n % half * BASE, (n % half + 1) * BASE)
        block = jnp.where(index == n // half, mine[place, :], other[place, :])
        target[i * BASE : (i + 1) * BASE, j * BASE : (j + 1) * BASE] = block
        if i != j:
            target[j * BASE : (j + 1) * BASE, i * BASE : (i + 1) * BASE] = block.T


def update_kernel(last, diag, low_a, low_b, high_a, high_b, both, link_b, both_low, both_high, next_b, new_diag, *rest):
    *new_both, low, high, link, nxt = rest
    index = lax.axis_index("blk")
    half = link_b.shape[1]
    unpack(low, low_a, low_b, index)
    unpack(high, high_a, high_b, index)
    join(link, both[:, :half], link_b, index)
    join(nxt, both_high[:, :half], next_b, index)
    mine = pl.ds(pl.multiple_of(index * half, half), half)
    low_pair = split(low[...])
    high_pair = split(high[...])
    link_pair = split(link[...])
    next_pair = split(nxt[...])
    link_rows = split(link[mine, :]) if last else link_pair
    next_columns = split(nxt[:, mine]) if last else next_pair
    old = diag[:, mine] if last else diag[...]
    gram = split(multiply(low_pair, link_rows, NT))
    upper = split(multiply(high_pair, next_columns))
    new_diag[...] = old + multiply(link_pair, gram) + multiply(next_pair, upper, TN)
    from_low = multiply(link_pair, split(multiply(low_pair, split(both_low[...]))))
    scaled_high = split(multiply(high_pair, split(both_high[:, half:])))
    right = both[:, half:] + from_low[:, half:] + multiply(next_pair, scaled_high, TN)
    if last:
        new_both[0][...] = from_low[:, :half]
        new_both[1][...] = right
    else:
        new_both[0][:, :half] = from_low[:, :half]
        new_both[0][:, half:] = right


def shifted(block, axis, distance):
    devices = range(lax.axis_size(axis))
    route = [(i - distance, i) for i in devices if i - distance in devices]
    return lax.ppermute(block, axis, route)


def swapped(block):
    return lax.ppermute(block, "blk", [(0, 1), (1, 0)])


def shards(hessian_part, coupling, rhs):
    order = coupling.shape[1]
    half = coupling.shape[2]
    section_index = lax.axis_index("hor")
    link = coupling[0]
    link = jnp.where(section_index >= 1, link, jnp.zeros_like(link))
    both = jnp.concatenate([link, rhs[0]], 1)
    width = both.shape[1]
    ins = [hessian_part[0], swapped(hessian_part[0])]
    for depth in range(LEVELS):
        last = depth == LEVELS - 1
        distance = 2**depth
        both_low = shifted(both, "hor", distance)
        both_high = shifted(both, "hor", -distance)
        diag, mine = invert(ins, order)
        mine = gated(mine, [both_low, both_high])
        link_other = swapped(both[:, :half])
        next_other = swapped(both_high[:, :half])
        low = shifted(mine, "hor", distance)
        high = shifted(mine, "hor", -distance)
        low_other = swapped(low)
        high_other = swapped(high)
        square = pltpu.VMEM((order, order), jnp.float32)
        args = [diag, low, low_other, high, high_other, both, link_other, both_low, both_high, next_other]
        outs = [(order, half), (order, half), (order, width - half)] if last else [(order, order), (order, width)]
        diag, *rest = local_call(functools.partial(update_kernel, last), args, outs, [square] * 4, 3 * 10**9, "update", 32)
        ins, both = [diag], rest[0]
    return (diag[None], rest[0][None], rest[1][None])


def solution(mesh):
    spec = P(("grp", "hor"), None, "blk")
    return jax.shard_map(
        shards,
        mesh=mesh,
        in_specs=(P(("grp", "hor"), "blk", None), spec, spec),
        out_specs=(spec, spec, spec),
        check_vma=False,
    )
```

```python
import functools

import jax
import jax.numpy as jnp
from jax import lax
from jax.experimental import pallas as pl
from jax.experimental.pallas import tpu as pltpu
from jax.sharding import PartitionSpec as P

LEVELS = 2
ROWS = 8
BASE = 128
NN = (((1,), (0,)), ((), ()))
NT = (((1,), (1,)), ((), ()))
TN = (((0,), (0,)), ((), ()))


def split(x):
    high = x.astype(jnp.bfloat16)
    return high, (x - high.astype(jnp.float32)).astype(jnp.bfloat16)


def multiply(a, b, dims=NN):
    dot = functools.partial(lax.dot_general, dimension_numbers=dims, preferred_element_type=jnp.float32)
    return dot(a[0], b[0]) + (dot(a[0], b[1]) + dot(a[1], b[0]))


def sweep_base(tiles):
    width = tiles[0].shape[1]
    shape = (ROWS, width)
    lane = lax.broadcasted_iota(jnp.int32, shape, 1)
    sub = lax.broadcasted_iota(jnp.int32, shape, 0)
    count = len(tiles)
    for p in range(count):
        first = p * ROWS
        block = tiles[p]
        columns = [
            [jnp.broadcast_to(tiles[q][:, first + l : first + l + 1], shape) for l in range(ROWS)]
            for q in range(p, min(p + 2, count))
        ]
        e = {
            (i, j): jnp.broadcast_to(columns[0][j][i : i + 1, :], shape) for i in range(ROWS) for j in range(i + 1)
        }
        at = lambda i, j: (max(i, j), min(i, j))
        for k in range(ROWS):
            inv = 1.0 / e[k, k]
            others = [i for i in range(ROWS) if i != k]
            col = {i: e[at(i, k)] for i in others}
            scaled = {i: col[i] * inv for i in others}
            for i in others:
                for j in others:
                    if j <= i:
                        e[i, j] = e[i, j] - scaled[i] * col[j]
            for i in others:
                e[at(i, k)] = scaled[i]
            e[k, k] = -inv
        negated = []
        for l in range(ROWS):
            value = e[at(0, l)]
            for i in range(1, ROWS):
                value = jnp.where(sub == i, e[at(i, l)], value)
            negated.append(value)
        rows = None
        for l in range(ROWS):
            term = negated[l] * jnp.broadcast_to(block[l : l + 1, :], shape)
            rows = -term if rows is None else rows - term
        for l in range(ROWS):
            rows = jnp.where(lane == first + l, negated[l], rows)
        spread = [jnp.broadcast_to(rows[l : l + 1, :], shape) for l in range(ROWS)]
        inside = (lane >= first) & (lane < first + ROWS)
        panel = jnp.concatenate([jnp.where(inside, tile, 0.0) for tile in tiles], 0)
        zero = jnp.zeros(shape, jnp.float32)
        padded = jnp.concatenate([rows if q == p else zero for q in range(count)], 0)
        delta = multiply(split(panel), split(padded))
        for q in range(count):
            if q == p:
                continue
            value = jnp.where(inside, 0.0, tiles[q])
            if q == p + 1:
                for l in range(ROWS):
                    value = value - columns[1][l] * spread[l]
            else:
                value = value - delta[q * ROWS : (q + 1) * ROWS, :]
            tiles[q] = value
        tiles[p] = rows
    return tiles


def sweep_all(work, base):
    order = work.shape[0]

    def step(k, carry):
        start = pl.multiple_of(k * BASE, BASE)
        tiles = [work[pl.ds(pl.multiple_of(start + r * ROWS, ROWS), ROWS), pl.ds(start, BASE)] for r in range(BASE // ROWS)]
        for r, tile in enumerate(sweep_base(tiles)):
            base[pl.ds(r * ROWS, ROWS), :] = tile
        negated = base[...]
        panel = split(work[:, pl.ds(start, BASE)])
        rows = -multiply(split(negated), split(work[pl.ds(start, BASE), :]))
        work[pl.ds(start, BASE), :] = rows
        work[pl.ds(start, BASE), pl.ds(start, BASE)] = negated
        rows = work[pl.ds(start, BASE), :]
        work[:, pl.ds(start, BASE)] = jnp.zeros((order, BASE), jnp.float32)
        work[...] = work[...] - multiply(panel, split(rows))
        work[pl.ds(start, BASE), :] = rows
        return carry

    lax.fori_loop(0, order // BASE, step, 0)


def lower_blocks(order):
    count = order // BASE
    return [(i, j) for i in range(count) for j in range(i + 1)]


def pack(out_ref, work):
    for n, (i, j) in enumerate(lower_blocks(work.shape[0])):
        out_ref[n * BASE : (n + 1) * BASE, :] = work[i * BASE : (i + 1) * BASE, j * BASE : (j + 1) * BASE]


def invert_pair_kernel(a_ref, b_ref, total_ref, out_ref, work, base):
    total_ref[...] = a_ref[...] + b_ref[...]
    work[...] = total_ref[...]
    sweep_all(work, base)
    pack(out_ref, work)


def invert_kernel(a_ref, out_ref, work, base):
    work[...] = a_ref[...]
    sweep_all(work, base)
    pack(out_ref, work)


def gate_kernel(*refs):
    pass


def gated(packed, others):
    return pl.pallas_call(
        gate_kernel,
        out_shape=jax.ShapeDtypeStruct(packed.shape, packed.dtype),
        in_specs=[pl.BlockSpec(memory_space=pl.ANY)] * (1 + len(others)),
        out_specs=pl.BlockSpec(memory_space=pl.ANY),
        input_output_aliases={0: 0},
        name="gate",
    )(packed, *others)


VMEM = pl.BlockSpec(memory_space=pltpu.VMEM)


def local_call(kernel, ins, outs, scratch, flops, name, mib):
    return pl.pallas_call(
        kernel,
        out_shape=[jax.ShapeDtypeStruct(s, jnp.float32) for s in outs],
        in_specs=[VMEM] * len(ins),
        out_specs=[VMEM] * len(outs),
        scratch_shapes=scratch,
        compiler_params=pltpu.CompilerParams(vmem_limit_bytes=mib * 2**20),
        cost_estimate=pl.CostEstimate(flops=flops, bytes_accessed=4 * 2**20, transcendentals=0),
        name=name,
    )(*ins)


def invert(ins, order):
    scratch = [pltpu.VMEM((order, order), jnp.float32), pltpu.VMEM((BASE, BASE), jnp.float32)]
    square = (order, order)
    packed = (len(lower_blocks(order)) * BASE, BASE)
    if len(ins) == 2:
        return local_call(invert_pair_kernel, ins, [square, packed], scratch, 40 * 10**9, "sum_invert", 12)
    return [ins[0], local_call(invert_kernel, ins, [packed], scratch, 40 * 10**9, "invert", 12)[0]]


def join(target, mine, other, index):
    half = mine.shape[1]
    for value, at in ((mine, index), (other, 1 - index)):
        target[:, pl.ds(pl.multiple_of(at * half, half), half)] = value[...]


def unpack(target, first, mine, other):
    for n, (i, j) in enumerate(lower_blocks(target.shape[0])):
        place = slice(n * BASE, (n + 1) * BASE)
        block = jnp.where(first, mine[place, :], other[place, :])
        target[i * BASE : (i + 1) * BASE, j * BASE : (j + 1) * BASE] = block
        if i != j:
            target[j * BASE : (j + 1) * BASE, i * BASE : (i + 1) * BASE] = block.T


def update_kernel(last, diag, mine_in, other_in, both, link_b, both_low, both_high, next_b, new_diag, *rest):
    *new_both, low, high, link, nxt = rest
    index = lax.axis_index("blk")
    half = link_b.shape[1]
    unpack(low, index == 0, mine_in, other_in)
    unpack(high, index == 1, mine_in, other_in)
    join(link, both[:, :half], link_b, index)
    join(nxt, both_high[:, :half], next_b, index)
    mine = pl.ds(pl.multiple_of(index * half, half), half)
    low_pair = split(low[...])
    high_pair = split(high[...])
    link_pair = split(link[...])
    next_pair = split(nxt[...])
    link_rows = split(link[mine, :]) if last else link_pair
    next_columns = split(nxt[:, mine]) if last else next_pair
    old = diag[:, mine] if last else diag[...]
    gram = split(multiply(low_pair, link_rows, NT))
    upper = split(multiply(high_pair, next_columns))
    new_diag[...] = old + multiply(link_pair, gram) + multiply(next_pair, upper, TN)
    from_low = multiply(link_pair, split(multiply(low_pair, split(both_low[...]))))
    scaled_high = split(multiply(high_pair, split(both_high[:, half:])))
    right = both[:, half:] + from_low[:, half:] + multiply(next_pair, scaled_high, TN)
    if last:
        new_both[0][...] = from_low[:, :half]
        new_both[1][...] = right
    else:
        new_both[0][:, :half] = from_low[:, :half]
        new_both[0][:, half:] = right


def shifted(block, axis, distance):
    devices = range(lax.axis_size(axis))
    route = [(i - distance, i) for i in devices if i - distance in devices]
    return lax.ppermute(block, axis, route)


def spread_both_ways(block, distance):
    count = lax.axis_size("hor")
    route = []
    for i in range(count):
        if i + distance < count:
            route += [(2 * i, 2 * (i + distance)), (2 * (i + distance) + 1, 2 * i + 1)]
    return lax.ppermute(block, ("hor", "blk"), route)


def swapped(block):
    return lax.ppermute(block, "blk", [(0, 1), (1, 0)])


def shards(hessian_part, coupling, rhs):
    order = coupling.shape[1]
    half = coupling.shape[2]
    section_index = lax.axis_index("hor")
    link = coupling[0]
    link = jnp.where(section_index >= 1, link, jnp.zeros_like(link))
    both = jnp.concatenate([link, rhs[0]], 1)
    width = both.shape[1]
    ins = [hessian_part[0], swapped(hessian_part[0])]
    for depth in range(LEVELS):
        last = depth == LEVELS - 1
        distance = 2**depth
        both_low = shifted(both, "hor", distance)
        both_high = shifted(both, "hor", -distance)
        link_other = swapped(both[:, :half])
        diag, mine = invert(ins, order)
        mine = gated(mine, [both_low, both_high, link_other])
        next_other = swapped(both_high[:, :half])
        mine = spread_both_ways(mine, distance)
        other = swapped(mine)
        square = pltpu.VMEM((order, order), jnp.float32)
        args = [diag, mine, other, both, link_other, both_low, both_high, next_other]
        outs = [(order, half), (order, half), (order, width - half)] if last else [(order, order), (order, width)]
        diag, *rest = local_call(functools.partial(update_kernel, last), args, outs, [square] * 4, 3 * 10**9, "update", 28)
        ins, both = [diag], rest[0]
    return (diag[None], rest[0][None], rest[1][None])


def solution(mesh):
    spec = P(("grp", "hor"), None, "blk")
    return jax.shard_map(
        shards,
        mesh=mesh,
        in_specs=(P(("grp", "hor"), "blk", None), spec, spec),
        out_specs=(spec, spec, spec),
        check_vma=False,
    )
```
